32 devices in a mesh: dom: 8 (over y, x, core), harm: 4 (over z).
Axes of the slice: x: 2, y: 2, z: 4, core: 2. Of those that a mesh axis runs over, the one named last changes fastest.
Arguments:
- basis: float32 [20, 2, 256, 16384], P(None, None, 'harm', 'dom'), may hold values from -200 to 200, as said below
- coeffs: float32 [20], replicated, may hold values from -4 to 4
- conductance_tiles: float32 [128, 6, 128, 128], P('dom'), may hold values from -0.21875 to 0.21875
- tile_cols: int32 [128, 6], P('dom'), may hold values from 0 to 23, as said below
- self_cond: float32 [16384], P('dom'), may hold values from 1.5 to 4
- cap: float32 [16384], P('dom'), may hold values from 0.05 to 0.5
- send_nodes: int32 [8, 8, 128], P('dom'), may hold values from 0 to 2047, as said below
- send_count: int32 [8, 8], P('dom'), may hold values from 0 to 128, as said below
- nl_nodes: int32 [8, 512], P('dom'), may hold values from 0 to 2047, as said below
- nl_count: int32 [8], P('dom'), may hold values from 1 to 512, 2048 in all
- op_wave: float32 [512, 4096], P(None, ('dom', 'harm')), may hold values from -1.5 to 1
- nl_gain: float32 [4096], P(('dom', 'harm')), may hold values from 0.1 to 1
Outputs:
- new_vector: float32 [2, 256, 16384], P(None, 'harm', 'dom')
- hess_column: float32 [21], replicated
The draws below stay inside these ranges and needn't reach their ends.
Inputs may be any that keep to these rules, and one draw needn't show every extreme that they name: `send_count`: A partition s lists live nodes only for the partitions 1, 7, 4 and 5 places after it (modulo 8), never for itself, at least 32 for each of those, and exactly 128 for at least one of them. `send_nodes`: distinct local nodes within one list. `tile_cols`: every tile of the ghost part of each partition's extended vector is read by some row tile of that partition. `nl_nodes`: distinct local nodes within a partition. The basis vectors are linearly independent.
All inputs are finite; a program needn't handle non-finite values. No bound on the sum of `nl_count` on one device may be relied on, other than what follows from the above.
Results may differ from the reference program's by a relative error of at most 0.0003.
Values sent between devices are 32-bit elements; how exact they have to be, the bound alone decides.
A program may use at most 128 MiB of HBM per device.

```python
import math
import jax
import jax.numpy as jnp
import numpy as np
from jax import lax

HARM = 256
BASIS = 20
TILE = 128
TPR = 6
PARTITION_NODES = 2048
PEER_CAP = 128
NL_CAP = 512
NL_MEAN = 256
NODES = 16384
NL_ALL = 4096
N_DOM = 8


def draw_basis(key, part):
    first, second = jax.random.split(jax.random.fold_in(key, 11), 2)
    shape_full = (BASIS, 2, HARM, NODES)
    node_frac = jnp.arange(NODES, dtype=jnp.float32) / NODES
    harm_frac = jnp.arange(HARM, dtype=jnp.float32) / HARM
    amplitude = jnp.sqrt(1.0 + 2.0 * node_frac)[None, None, None, :] * jnp.sqrt(1.0 + 2.0 * harm_frac)[None, None, :, None]
    rough = jnp.clip(jax.random.normal(first, shape_full, jnp.float32), -6.0, 6.0)
    common = jnp.clip(jax.random.normal(second, (1, 2, HARM, NODES), jnp.float32), -6.0, 6.0)
    return (rough + 0.7 * common) * amplitude


def draw_tile_cols(key, part):
    first, second = jax.random.split(jax.random.fold_in(key, 17))
    local_tiles = PARTITION_NODES // TILE
    ghost_tiles = N_DOM * PEER_CAP // TILE
    tile_index = jnp.arange(NODES // TILE, dtype=jnp.int32)
    within = tile_index % local_tiles
    owner = tile_index // local_tiles
    offsets = jax.random.randint(first, (N_DOM,), 0, ghost_tiles)[owner]
    last_col = jax.random.randint(second, (NODES // TILE,), 0, local_tiles)
    columns = [within]
    for index in range(TPR - 2):
        columns.append(local_tiles + ((TPR - 2) * within + index + offsets) % ghost_tiles)
    columns.append(last_col)
    return jnp.stack(columns, axis=1).astype(jnp.int32)


def draw_send_nodes(key, part):
    keys = jax.random.split(jax.random.fold_in(key, 21), N_DOM * N_DOM)
    chosen = jax.vmap(lambda single: jax.random.permutation(single, PARTITION_NODES)[:PEER_CAP])(keys)
    return chosen.reshape(N_DOM, N_DOM, PEER_CAP).astype(jnp.int32)


def draw_send_count(key, part):
    first, second = jax.random.split(jax.random.fold_in(key, 31))
    counts = jax.random.randint(first, (N_DOM, N_DOM), PEER_CAP // 4, PEER_CAP + 1)
    sender = jnp.arange(N_DOM, dtype=jnp.int32)
    offsets = jnp.array([1, N_DOM - 1, N_DOM // 2, N_DOM // 2 + 1], dtype=jnp.int32)
    distance = (sender[None, :] - sender[:, None]) % N_DOM
    near = jnp.any(distance[:, :, None] == offsets[None, None, :], axis=2)
    choose = jax.random.randint(second, (N_DOM,), 0, 2)
    jumps = jnp.where(choose == 0, 1, N_DOM // 2)
    full = distance == jumps[:, None]
    counts = jnp.where(near, counts, 0)
    counts = jnp.where(full, PEER_CAP, counts)
    counts = jnp.where(distance == 0, 0, counts)
    return counts.astype(jnp.int32)


def draw_nl_nodes(key, part):
    keys = jax.random.split(jax.random.fold_in(key, 41), N_DOM)
    chosen = jax.vmap(lambda single: jax.random.permutation(single, PARTITION_NODES)[:NL_CAP])(keys)
    return chosen.astype(jnp.int32)


def steps_of(key, shape, cuts, smallest, largest):
    def one(position, blocks):
        steps = jax.random.uniform(jax.random.fold_in(jax.random.fold_in(key, 6), position), (blocks,), jnp.float32, smallest / len(cuts), largest / len(cuts))
        return jnp.repeat(jnp.exp(steps), shape[position] // blocks).reshape((-1,) + (1,) * (len(shape) - position - 1))

    loudness = one(*cuts[0])
    for cut in cuts[1:]:
        loudness = loudness * one(*cut)
    return loudness


def length_profile(count, total, limit, skew):
    loads = [(1 << 20) // math.isqrt(standing ** skew) + 1 for standing in range(2, count + 1)]
    rest, holding = total - limit - (count - 1), [1] * (count - 1)
    while rest > 0:
        movable = [i for i in range(count - 1) if holding[i] < limit]
        whole, left = sum([loads[i] for i in movable]), rest
        for i in movable:
            more = min(limit - holding[i], max(1, left * loads[i] // whole), rest)
            holding[i] = holding[i] + more
            rest = rest - more
    return np.array([limit] + holding)


def uneven_parts(own_key, count, total, most, lean):
    if count == 2:
        one = jax.random.randint(own_key, (), max(1, total - most), min(most, total - 1) + 1)
        return jnp.stack([one, total - one])
    lengths = jnp.asarray(length_profile(count, total, most, lean), jnp.int32)
    twos = (count - 1) // 2
    source_of, taker = lengths[1:1 + 2 * twos:2], lengths[2:2 + 2 * twos:2]
    room = jnp.minimum(source_of - 1, most - taker)
    shifted = jax.random.randint(jax.random.fold_in(own_key, 1), (twos,), 0, 1 << 20) % (room + 1)
    lengths = lengths.at[1:1 + 2 * twos:2].set(source_of - shifted).at[2:2 + 2 * twos:2].set(taker + shifted)
    return lengths[jax.random.permutation(jax.random.fold_in(own_key, 2), count)]


def gaussian(own_key, shape, width, limit, cuts=(), held_as=jnp.bfloat16):
    result = jax.random.normal(own_key, shape, jnp.float32) * width
    if len(cuts) > 0:
        result = steps_of(own_key, shape, cuts, -0.22, 0.18) * result
    return jnp.clip(result, min=-limit, max=limit).astype(held_as)


def setup_inputs(seed: int = 0) -> dict:
    seeds = jax.random.split(jax.random.key(seed), 13)
    return {
        "basis": draw_basis(jax.random.fold_in(seeds[12], 71), 0),
        "coeffs": gaussian(seeds[1], (BASIS,), 1.0, 4.0, (), jnp.float32),
        "conductance_tiles": gaussian(seeds[2], (NODES // TILE, TPR, TILE, TILE), (TPR * TILE) ** -0.5, 0.21875, ((0, 8),), jnp.float32),
        "tile_cols": draw_tile_cols(jax.random.fold_in(seeds[12], 71), 0),
        "self_cond": jnp.clip(jnp.exp(math.log(4.0) - 0.98082925 * jax.random.uniform(seeds[4], (NODES,), jnp.float32) ** steps_of(seeds[4], (NODES,), ((0, 8),), -0.2, 0.2)), 1.5, 4.0),
        "cap": jnp.clip(jnp.exp(math.log(0.5) - 2.3025851 * jax.random.uniform(seeds[5], (NODES,), jnp.float32) ** steps_of(seeds[5], (NODES,), ((0, 8),), -0.2, 0.2)), 0.05, 0.5),
        "send_nodes": draw_send_nodes(jax.random.fold_in(seeds[12], 71), 0),
        "send_count": draw_send_count(jax.random.fold_in(seeds[12], 71), 0),
        "nl_nodes": draw_nl_nodes(jax.random.fold_in(seeds[12], 71), 0),
        "nl_count": uneven_parts(seeds[9], N_DOM, N_DOM * NL_MEAN, NL_CAP, 2).astype(jnp.int32),
        "op_wave": jnp.clip(-1.5 + 2.5 * jax.random.uniform(seeds[10], (2 * HARM, NL_ALL), jnp.float32) ** steps_of(seeds[10], (2 * HARM, NL_ALL), ((1, 32),), -0.2, 0.2), -1.5, 1.0),
        "nl_gain": jnp.clip(jnp.exp(math.log(1.0) - 2.3025851 * jax.random.uniform(seeds[11], (NL_ALL,), jnp.float32) ** steps_of(seeds[11], (NL_ALL,), ((0, 32),), -0.2, 0.2)), 0.1, 1.0),
    }


epsilon = 1e-06

def tables(harmonic, samples):
    sample_index = jnp.arange(samples, dtype=jnp.int32)
    product = harmonic[None, :] * sample_index[:, None] % samples
    angles = 2.0 * math.pi * product.astype(jnp.float32) / samples
    cosine = jnp.cos(angles)
    sine_part = jnp.sin(angles)
    alternating = 1.0 - 2.0 * (sample_index % 2).astype(jnp.float32)
    is_zero = harmonic == 0
    second = jnp.where(is_zero[None, :], alternating[:, None], sine_part)
    inverse = jnp.stack([cosine, second], axis=1)
    weights = jnp.where(is_zero, 1.0 / samples, 2.0 / samples).astype(jnp.float32)
    forward = jnp.transpose(jnp.stack([cosine * weights[None, :], second * weights[None, :]], axis=1), (1, 2, 0))
    return (inverse, forward)

def solve_gram(gram_matrix, projections):
    factor = jnp.linalg.cholesky(gram_matrix)
    size_count = gram_matrix.shape[0]
    middle = jnp.zeros_like(projections)
    for index in range(size_count):
        middle = middle.at[index].set((projections[index] - jnp.dot(factor[index], middle, precision=lax.Precision.HIGHEST)) / factor[index, index])
    answer = jnp.zeros_like(projections)
    for index in range(size_count - 1, -1, -1):
        answer = answer.at[index].set((middle[index] - jnp.dot(factor[:, index], answer, precision=lax.Precision.HIGHEST)) / factor[index, index])
    return answer

def reference(basis, coeffs, conductance_tiles, tile_cols, self_cond, cap, send_nodes, send_count, nl_nodes, nl_count, op_wave, nl_gain):
    highest_harmonic = lax.Precision.HIGHEST
    count_of_rows = 2 * HARM
    vector = jnp.einsum('b,bpkn->pkn', coeffs, basis, precision=highest_harmonic)
    flattened = vector.reshape(count_of_rows, NODES)
    local_tiles = PARTITION_NODES // TILE
    slot_index = jnp.arange(PEER_CAP, dtype=jnp.int32)
    part_index = jnp.arange(N_DOM, dtype=jnp.int32)

    def one_part(receiver):
        listed = lax.dynamic_index_in_dim(send_nodes, receiver, 1, keepdims=False)
        live_counts = lax.dynamic_index_in_dim(send_count, receiver, 1, keepdims=False)
        active = slot_index[None, :] < live_counts[:, None]
        node_index = (listed + part_index[:, None] * PARTITION_NODES).reshape(-1)
        ghosts = jnp.take(flattened, node_index, axis=1).reshape(count_of_rows, N_DOM, PEER_CAP)
        ghosts = jnp.where(active[None], ghosts, 0.0)
        own_block = lax.dynamic_slice_in_dim(flattened, receiver * PARTITION_NODES, PARTITION_NODES, 1).reshape(count_of_rows, local_tiles, TILE)
        extended = jnp.concatenate([own_block, ghosts.reshape(count_of_rows, -1, TILE)], axis=1)
        columns = lax.dynamic_slice_in_dim(tile_cols, receiver * local_tiles, local_tiles, 0)
        node_conductance = lax.dynamic_slice_in_dim(conductance_tiles, receiver * local_tiles, local_tiles, 0)
        picked_entries = jnp.take(extended, columns, axis=1)
        return jnp.einsum('rhfq,hfqo->rho', picked_entries, node_conductance, precision=highest_harmonic).reshape(count_of_rows, PARTITION_NODES)
    coupled_nodes = lax.map(one_part, part_index)
    coupled_nodes = jnp.transpose(coupled_nodes, (1, 0, 2)).reshape(2, HARM, NODES)
    harmonic = jnp.arange(HARM, dtype=jnp.int32)
    angular = 2.0 * math.pi * harmonic.astype(jnp.float32) / HARM
    frequency = jnp.stack([-angular[:, None] * cap[None, :] * vector[1], angular[:, None] * cap[None, :] * vector[0]])
    base = coupled_nodes + self_cond[None, None, :] * vector + frequency
    nl_index = (nl_nodes + part_index[:, None] * PARTITION_NODES).reshape(-1)
    nl_active = (jnp.arange(NL_CAP, dtype=jnp.int32)[None, :] < nl_count[:, None]).reshape(-1)
    sampled = jnp.where(nl_active[None, :], jnp.take(flattened, nl_index, axis=1), 0.0)
    inverse, forward = tables(harmonic, count_of_rows)
    waveform = jnp.dot(inverse.reshape(count_of_rows, count_of_rows), sampled, precision=highest_harmonic)
    current = nl_gain[None, :] * jnp.exp(op_wave) * waveform
    returned = jnp.dot(forward.reshape(count_of_rows, count_of_rows), current, precision=highest_harmonic)
    returned = jnp.where(nl_active[None, :], returned, 0.0)
    product = base.reshape(count_of_rows, NODES).at[:, nl_index].add(returned).reshape(2, HARM, NODES)
    entries = 2 * HARM * NODES
    gram_matrix = jnp.einsum('apkn,bpkn->ab', basis, basis, precision=highest_harmonic) / entries
    projections = jnp.einsum('apkn,pkn->a', basis, product, precision=highest_harmonic) / entries
    hess = solve_gram(gram_matrix, projections)
    residual = product - jnp.einsum('a,apkn->pkn', hess, basis, precision=highest_harmonic)
    mean_square = jnp.sum(residual * residual) / entries
    norm_value = jnp.sqrt(mean_square + epsilon)
    return (residual / norm_value, jnp.concatenate([hess, norm_value[None]]))
```

```python
import functools
import math

import jax
import jax.numpy as jnp
import ml_dtypes
import numpy as np
from jax import lax
from jax.experimental import pallas as pl
from jax.experimental.pallas import tpu as pltpu
from jax.sharding import PartitionSpec as P

epsilon = 1e-06
BF = jnp.bfloat16
F32 = jnp.float32
HI = lax.Precision.HIGHEST
NT = (((1,), (1,)), ((), ()))


def dft_tables(groups, harm_local):
    harm = groups * harm_local
    samples = 2 * harm
    n = np.arange(samples)[:, None]
    k = np.arange(harm)[None, :]
    angle = 2.0 * np.pi * ((n * k) % samples) / samples
    cosine, sine = np.cos(angle), np.sin(angle)
    sine[:, 0] = 1.0 - 2.0 * (np.arange(samples) % 2)
    inverse = np.stack(
        [cosine.reshape(samples, groups, harm_local), sine.reshape(samples, groups, harm_local)],
        axis=2,
    ).reshape(samples, samples)
    weight = np.full((harm,), 2.0 / samples)
    weight[0] = 1.0 / samples
    weight = np.broadcast_to(
        weight.reshape(groups, 1, harm_local), (groups, 2, harm_local)
    ).reshape(samples)
    forward = (inverse * weight[None, :]).T

    def split(x):
        x = x.astype(np.float32)
        high = x.astype(ml_dtypes.bfloat16)
        low = (x - high.astype(np.float32)).astype(ml_dtypes.bfloat16)
        return [high, low]

    return np.stack(split(inverse) + split(forward))


def split2(x):
    high = x.astype(BF)
    return high, (x - high.astype(F32)).astype(BF)


def kernel(
    dims,
    basis_hbm, cond_hbm, wave_hbm, table_hbm, coef, cols, scount, ncount,
    selfc, cap, snodes, nnodes, gain,
    out_hbm, hess_ref,
    bv, cv, wv, tv, vec, ext_h, ext_l, oh, sacc, xs, xr, rs, rr, gs, gr, prod, outv,
    gmat, g1, g2, p1, p2, g2s, p2s, hspl,
    in_sem, aux_sem, out_sem,
    xs_sem, xr_sem, rs_sem, rr_sem, gs_sem, gr_sem,
    g1s_sem, g1r_sem, g2s_sem, g2r_sem, p1s_sem, p1r_sem, p2s_sem, p2r_sem,
):
    B, R, ND, NL, H, D, T, TPR, TILE, CAP = dims
    HL, SL = R // 2, NL // H
    RT = R * H
    CH = 256
    NCH = ND // CH
    offs = (1, D - 1, D // 2, D // 2 + 1)
    md = lax.axis_index("dom")
    mh = lax.axis_index("harm")
    entries = float(R * H * ND * D)

    def bcopy(c):
        lanes = pl.ds(pl.multiple_of(c * CH, CH), CH)
        return pltpu.make_async_copy(
            basis_hbm.at[:, :, lanes], bv.at[:, :, lanes], in_sem.at[c]
        )

    for c in range(NCH):
        bcopy(c).start()
    wcopy = pltpu.make_async_copy(wave_hbm, wv, aux_sem.at[0])
    tcopy = pltpu.make_async_copy(table_hbm, tv, aux_sem.at[1])
    ccopy = pltpu.make_async_copy(cond_hbm, cv, aux_sem.at[2])
    tcopy.start()
    wcopy.start()
    ccopy.start()

    dpeers = [lax.rem(md + j, D) for j in range(1, D)]
    hpeers = [lax.rem(mh + j, H) for j in range(1, H)]
    barrier = pltpu.get_barrier_semaphore()
    for p in dpeers:
        pl.semaphore_signal(barrier, inc=1, device_id=(p, mh), device_id_type=pl.DeviceIdType.MESH)
    for p in hpeers:
        pl.semaphore_signal(barrier, inc=1, device_id=(md, p), device_id_type=pl.DeviceIdType.MESH)

    lane = lax.broadcasted_iota(jnp.int32, (1, NL), 1)
    heads = [jnp.where(lane < ncount[0], nnodes[...], -1)]
    lane = lax.broadcasted_iota(jnp.int32, (1, CAP), 1)
    for off in offs:
        p = lax.rem(md + off, D)
        heads.append(jnp.where(lane < scount[0, p], snodes[pl.ds(p, 1), :], -1))
    head = jnp.concatenate(heads, axis=1)
    W = NL + 4 * CAP

    def build(c, carry):
        rows = lax.broadcasted_iota(jnp.int32, (64, W), 0) + c * 64
        oh[pl.ds(pl.multiple_of(c * 64, 64), 64), :] = jnp.where(rows == head, 1.0, 0.0).astype(BF)
        return carry

    lax.fori_loop(0, ND // 64, build, 0)
    for s in range(D):
        ext_h[T + s] = jnp.zeros((R, TILE), BF)
        ext_l[T + s] = jnp.zeros((R, TILE), BF)
    sacc[...] = jnp.zeros_like(sacc)

    def chunk(c, carry):
        bcopy(c).wait()
        lanes = pl.ds(pl.multiple_of(c * CH, CH), CH)

        def rows_step(r, carry2):
            rows = pl.ds(pl.multiple_of(r * 32, 32), 32)
            acc = coef[0] * bv[0, rows, lanes]
            for b in range(1, B):
                acc = acc + coef[b] * bv[b, rows, lanes]
            high, low = split2(acc)
            for i in range(CH // TILE):
                cut = slice(i * TILE, (i + 1) * TILE)
                vec[c * (CH // TILE) + i, rows, :] = acc[:, cut]
                ext_h[c * (CH // TILE) + i, rows, :] = high[:, cut]
                ext_l[c * (CH // TILE) + i, rows, :] = low[:, cut]
            return carry2

        lax.fori_loop(0, R // 32, rows_step, 0)
        high = jnp.concatenate([ext_h[c * 2], ext_h[c * 2 + 1]], axis=1)
        low = jnp.concatenate([ext_l[c * 2], ext_l[c * 2 + 1]], axis=1)
        both = jnp.concatenate([high, low], axis=0)
        got = jnp.dot(both, oh[lanes, :], preferred_element_type=F32)
        sacc[...] += got[:R] + got[R:]
        return carry

    lax.fori_loop(0, NCH, chunk, 0)

    pl.semaphore_wait(barrier, D - 1 + H - 1)

    def hcopy(src, dst, ssem, rsem, peer, slot):
        return pltpu.make_async_remote_copy(
            src_ref=src, dst_ref=dst.at[slot], send_sem=ssem.at[peer], recv_sem=rsem.at[slot],
            device_id=(md, peer), device_id_type=pl.DeviceIdType.MESH,
        )

    def dcopy(src, dst, ssem, rsem, peer, slot):
        return pltpu.make_async_remote_copy(
            src_ref=src, dst_ref=dst.at[slot], send_sem=ssem.at[peer], recv_sem=rsem.at[slot],
            device_id=(peer, mh), device_id_type=pl.DeviceIdType.MESH,
        )

    for h in range(H):
        xs[h] = sacc[:, h * SL:(h + 1) * SL]
    for p in hpeers:
        hcopy(xs.at[p], xr, xs_sem, xr_sem, p, mh).start()
    xr[mh] = xs[mh]

    def gcopy(j, off):
        return pltpu.make_async_remote_copy(
            src_ref=gs.at[j], dst_ref=gr.at[j], send_sem=gs_sem.at[j], recv_sem=gr_sem.at[j],
            device_id=(lax.rem(md + off, D), mh), device_id_type=pl.DeviceIdType.MESH,
        )

    for j, off in enumerate(offs):
        gs[j] = sacc[:, NL + j * CAP:NL + (j + 1) * CAP]
        gcopy(j, off).start()

    BG = 8 * B
    gmat[...] = jnp.zeros_like(gmat)

    def gram_step(g, carry):
        x = bv[:, pl.ds(pl.multiple_of(g * 8, 8), 8), :].reshape(BG, ND)
        high, low = split2(x)
        both = jnp.concatenate([high, low], axis=0)
        gmat[...] += lax.dot_general(high, both, NT, preferred_element_type=F32)
        return carry

    lax.fori_loop(0, R // 8, gram_step, 0)
    row = lax.broadcasted_iota(jnp.int32, (BG, BG), 0)
    col = lax.broadcasted_iota(jnp.int32, (BG, BG), 1)
    same = row % 8 == col % 8
    hh = jnp.where(same, gmat[:, :BG], 0.0)
    hl = jnp.where(same, gmat[:, BG:], 0.0)
    r2 = lax.broadcasted_iota(jnp.int32, (128, BG), 0)
    c2 = lax.broadcasted_iota(jnp.int32, (128, BG), 1)
    pick = jnp.where(r2 == c2 // 8, 1.0, 0.0)
    top = pick[:32]
    mid = jnp.dot(top, hh + hl, precision=HI, preferred_element_type=F32)
    mid = mid + lax.dot_general(top, hl, NT, precision=HI, preferred_element_type=F32)
    g1[md] = lax.dot_general(mid, pick, NT, precision=HI, preferred_element_type=F32)
    for p in dpeers:
        dcopy(g1.at[md], g1, g1s_sem, g1r_sem, p, md).start()

    wcopy.wait()
    tcopy.wait()
    wv[...] = gain[...] * jnp.exp(wv[...])

    for p in hpeers:
        hcopy(xs.at[p], xr, xs_sem, xr_sem, p, p).wait_recv()

    def transform(high_table, low_table, x):
        high, low = split2(x)
        both = jnp.concatenate([high, low], axis=1)
        y = jnp.dot(high_table, both, preferred_element_type=F32)
        z = jnp.dot(low_table, high, preferred_element_type=F32)
        return y[:, :SL] + y[:, SL:] + z

    waves = transform(tv[0], tv[1], xr[...].reshape(RT, SL))
    back = transform(tv[2], tv[3], wv[...] * waves)
    rs[...] = back.reshape(H, R, SL)
    for p in hpeers:
        hcopy(rs.at[p], rr, rs_sem, rr_sem, p, mh).start()
    rr[mh] = rs[mh]

    for p in dpeers:
        dcopy(g1.at[md], g1, g1s_sem, g1r_sem, p, p).wait_recv()
    g2[mh] = jnp.sum(g1[...], axis=0)
    for p in hpeers:
        hcopy(g2.at[mh], g2, g2s_sem, g2r_sem, p, mh).start()

    ccopy.wait()
    for j, off in enumerate(offs):
        gcopy(j, off).wait_recv()
        high, low = split2(gr[j])
        src = lax.rem(md + (D - off), D)
        ext_h[T + src] = high
        ext_l[T + src] = low
    harmonic = lax.broadcasted_iota(jnp.int32, (HL, TILE), 0) + mh * HL
    omega = 2.0 * math.pi * harmonic.astype(F32) / float(HL * H)

    def tile_step(t, carry):
        nodes = pl.ds(pl.multiple_of(t * TILE, TILE), TILE)
        highs = [ext_h[cols[t, i]] for i in range(TPR)]
        lows = [ext_l[cols[t, i]] for i in range(TPR)]
        both = jnp.concatenate(
            [jnp.concatenate(highs, axis=1), jnp.concatenate(lows, axis=1)], axis=0
        )
        ch, cl = split2(cv[t].reshape(TPR * TILE, TILE))
        y = jnp.dot(both, jnp.concatenate([ch, cl], axis=1), preferred_element_type=F32)
        y = y[:R] + y[R:]
        y = y[:, :TILE] + y[:, TILE:]
        v = vec[t]
        y = y + selfc[:, nodes] * v
        turn = omega * cap[:, nodes]
        prod[0:HL, nodes] = y[:HL] - turn * v[HL:]
        prod[HL:R, nodes] = y[HL:] + turn * v[:HL]
        return carry

    lax.fori_loop(0, T, tile_step, 0)

    for p in hpeers:
        hcopy(g2.at[mh], g2, g2s_sem, g2r_sem, p, p).wait_recv()
    ri = lax.broadcasted_iota(jnp.int32, (32, 128), 0)
    ci = lax.broadcasted_iota(jnp.int32, (32, 128), 1)
    work = jnp.sum(g2[...], axis=0) / entries + jnp.where((ci == ri + 64) & (ri < B), 1.0, 0.0)
    diag = jnp.ones((32, 1), F32)
    for k in range(B):
        pivot = work[k:k + 1, k:k + 1]
        diag = jnp.where(ri[:, :1] == k, pivot, diag)
        factor = jnp.where(ri[:, :1] > k, work[:, k:k + 1] / pivot, 0.0)
        work = work - factor * work[k:k + 1, :]
    lower = jnp.concatenate([work[:, 64:], jnp.zeros((32, 64), F32)], axis=1)

    for p in hpeers:
        hcopy(rs.at[p], rr, rs_sem, rr_sem, p, p).wait_recv()
    rh, rl = split2(jnp.concatenate([rr[h] for h in range(H)], axis=1))
    both = jnp.concatenate([rh, rl], axis=0)

    def add_step(c, carry):
        lanes = pl.ds(pl.multiple_of(c * CH, CH), CH)
        y = lax.dot_general(both, oh[lanes, :NL], NT, preferred_element_type=F32)
        prod[:, lanes] += y[:R] + y[R:]
        return carry

    lax.fori_loop(0, NCH, add_step, 0)

    def fold(x):
        parts = [x[:, i * 128:(i + 1) * 128] for i in range(x.shape[1] // 128)]
        while len(parts) > 1:
            parts = [a + b for a, b in zip(parts[::2], parts[1::2])]
        return parts[0]

    def proj_step(g, carry):
        rows = pl.ds(pl.multiple_of(g * 8, 8), 8)
        p = prod[rows, :]
        new = [carry[b] + fold(bv[b, rows, :] * p) for b in range(B)]
        new.append(carry[B] + fold(p * p))
        return tuple(new)

    accs = lax.fori_loop(0, R // 8, proj_step, tuple(jnp.zeros((8, 128), F32) for _ in range(B + 1)))
    sums = [jnp.sum(a, axis=0, keepdims=True) for a in accs]
    stack = jnp.concatenate(sums + [jnp.zeros((128 - B - 1, 128), F32)], axis=0)
    p1[md] = lax.dot_general(jnp.ones((8, 128), F32), stack, NT, precision=HI, preferred_element_type=F32)
    for p in dpeers:
        dcopy(p1.at[md], p1, p1s_sem, p1r_sem, p, md).start()
    for p in dpeers:
        dcopy(p1.at[md], p1, p1s_sem, p1r_sem, p, p).wait_recv()
    p2[mh] = jnp.sum(p1[...], axis=0)
    for p in hpeers:
        hcopy(p2.at[mh], p2, p2s_sem, p2r_sem, p, mh).start()
    for p in hpeers:
        hcopy(p2.at[mh], p2, p2s_sem, p2r_sem, p, p).wait_recv()
    total = jnp.sum(p2[...], axis=0)[:1] / entries
    li = ci[:1]
    energy = jnp.sum(jnp.where(li == B, total, 0.0), axis=1, keepdims=True)
    proj = jnp.where(li < B, total, 0.0)
    y = jnp.sum(lower * proj, axis=1, keepdims=True)
    z = y / diag
    hess = jnp.sum(lower * z, axis=0, keepdims=True)
    square = energy - jnp.sum(proj * hess, axis=1, keepdims=True)
    norm = jnp.sqrt(square + epsilon)
    hess_ref[...] = jnp.where(li == B, norm, hess)
    for b in range(B):
        one = jnp.sum(jnp.where(li == b, hess, 0.0), axis=1, keepdims=True)
        hspl[b] = jnp.broadcast_to(one, (8, 128))
    hspl[B] = jnp.broadcast_to(1.0 / norm, (8, 128))

    WIDE = 1024
    scale = jnp.concatenate([hspl[B]] * (WIDE // 128), axis=1)

    def ocopy(q):
        rows = pl.ds(pl.multiple_of(q * 16, 16), 16)
        return pltpu.make_async_copy(outv.at[rows, :], out_hbm.at[rows, :], out_sem.at[q])

    def out_step(q, carry):
        for i in range(2):
            rows = pl.ds(pl.multiple_of(q * 16 + i * 8, 8), 8)
            for w in range(ND // WIDE):
                cut = slice(w * WIDE, (w + 1) * WIDE)
                acc = prod[rows, cut]
                for b in range(B):
                    acc = acc - jnp.concatenate([hspl[b]] * (WIDE // 128), axis=1) * bv[b, rows, cut]
                outv[rows, cut] = acc * scale
        ocopy(q).start()
        return carry

    lax.fori_loop(0, R // 16, out_step, 0)

    for p in hpeers:
        hcopy(xs.at[p], xr, xs_sem, xr_sem, p, mh).wait_send()
        hcopy(rs.at[p], rr, rs_sem, rr_sem, p, mh).wait_send()
        hcopy(g2.at[mh], g2, g2s_sem, g2r_sem, p, mh).wait_send()
        hcopy(p2.at[mh], p2, p2s_sem, p2r_sem, p, mh).wait_send()
    for p in dpeers:
        dcopy(g1.at[md], g1, g1s_sem, g1r_sem, p, md).wait_send()
        dcopy(p1.at[md], p1, p1s_sem, p1r_sem, p, md).wait_send()
    for j, off in enumerate(offs):
        gcopy(j, off).wait_send()
    for q in range(R // 16):
        ocopy(q).wait()


def local(
    basis, coeffs, conductance_tiles, tile_cols, self_cond, cap,
    send_nodes, send_count, nl_nodes, nl_count, op_wave, nl_gain,
):
    B, _, HL, ND = basis.shape
    R = 2 * HL
    T, TPR, TILE, _ = conductance_tiles.shape
    D, CAP = send_nodes.shape[1:]
    NL = nl_nodes.shape[1]
    H = lax.axis_size("harm")
    SL = NL // H
    S = R * H
    dims = (B, R, ND, NL, H, D, T, TPR, TILE, CAP)
    table = jnp.asarray(dft_tables(H, HL))
    any_ = pl.BlockSpec(memory_space=pl.ANY)
    vmem = pl.BlockSpec(memory_space=pltpu.VMEM)
    smem = pl.BlockSpec(memory_space=pltpu.SMEM)
    dma = pltpu.SemaphoreType.DMA
    V = pltpu.VMEM
    out, column = pl.pallas_call(
        functools.partial(kernel, dims),
        out_shape=(
            jax.ShapeDtypeStruct((R, ND), F32),
            jax.ShapeDtypeStruct((1, 128), F32),
        ),
        in_specs=[any_] * 4 + [smem] * 4 + [vmem] * 5,
        out_specs=(any_, vmem),
        scratch_shapes=[
            V((B, R, ND), F32),
            V(conductance_tiles.shape, F32),
            V((S, SL), F32),
            V((4, S, S), BF),
            V((T, R, TILE), F32),
            V((T + D, R, TILE), BF),
            V((T + D, R, TILE), BF),
            V((ND, NL + 4 * CAP), BF),
            V((R, NL + 4 * CAP), F32),
            V((H, R, SL), F32),
            V((H, R, SL), F32),
            V((H, R, SL), F32),
            V((H, R, SL), F32),
            V((4, R, CAP), F32),
            V((4, R, CAP), F32),
            V((R, ND), F32),
            V((R, ND), F32),
            V((8 * B, 16 * B), F32),
            V((D, 32, 128), F32),
            V((H, 32, 128), F32),
            V((D, 8, 128), F32),
            V((H, 8, 128), F32),
            V((8, 128), F32),
            V((8, 128), F32),
            V((B + 1, 8, 128), F32),
            dma((ND // 256,)), dma((3,)), dma((R // 16,)),
            dma((H,)), dma((H,)), dma((H,)), dma((H,)), dma((4,)), dma((4,)),
            dma((D,)), dma((D,)), dma((H,)), dma((H,)),
            dma((D,)), dma((D,)), dma((H,)), dma((H,)),
        ],
        compiler_params=pltpu.CompilerParams(
            collective_id=0, has_side_effects=True, vmem_limit_bytes=58 * 2**20
        ),
    )(
        basis.reshape(B, R, ND),
        conductance_tiles,
        op_wave,
        table,
        coeffs,
        tile_cols,
        send_count,
        nl_count,
        self_cond.reshape(1, ND),
        cap.reshape(1, ND),
        send_nodes.reshape(D, CAP),
        nl_nodes,
        nl_gain.reshape(1, SL),
    )
    return out.reshape(2, HL, ND), column[0, :B + 1]


def solution(mesh):
    in_specs = (
        P(None, None, "harm", "dom"),
        P(),
        P("dom", None, None, None),
        P("dom", None),
        P("dom"),
        P("dom"),
        P("dom", None, None),
        P("dom", None),
        P("dom", None),
        P("dom"),
        P(None, ("dom", "harm")),
        P(("dom", "harm")),
    )
    out_specs = (P(None, "harm", "dom"), P())
    return jax.shard_map(local, mesh=mesh, in_specs=in_specs, out_specs=out_specs, check_vma=False)
```
